512 devices in a mesh: view: 8 (over z_hi, y), seq: 64 (over z_lo, x, core).
Axes of the slice: x: 4, y: 4, z: 16 (z_hi: 2, z_lo: 8; z = z_hi * 8 + z_lo), core: 2. Of those that a mesh axis runs over, the one named last changes fastest.
Arguments:
- queries: bfloat16 [4, 8, 2048, 2048], P(None, 'view', 'seq'), may hold values from -6 to 6
- key_rows: bfloat16 [4, 8, 2048, 2048], P(None, 'view', 'seq'), may hold values from -6 to 6
- value_rows: bfloat16 [4, 8, 2048, 2048], P(None, 'view', 'seq'), may hold values from -6 to 6
- view_queries: bfloat16 [4, 8, 2048, 2048], P(None, 'view', 'seq'), may hold values from -6 to 6
Outputs:
- spatial: bfloat16 [4, 8, 2048, 2048], P(None, 'view', 'seq')
- joined: bfloat16 [4, 8, 2048, 2048], P(None, 'view', 'seq')
The draws below stay inside these ranges and needn't reach their ends.
All inputs are finite; a program needn't handle non-finite values.
Results may differ from the reference program's by a relative error of at most 0.0064.
Values may be sent and summed in bfloat16 or wider, within the bound.
A program may use at most 64 MiB of HBM per device.

```python
import jax
import jax.numpy as jnp
from jax import lax

HEADS = 32
HEAD_DIM = 64
D = 2048
BATCH = 4
SEQ_LEN = 2048
VIEWS = 8


def draw_queries(key, part):
    key = jax.random.fold_in(key, 1)
    full_shape = (BATCH, VIEWS, SEQ_LEN, HEADS, HEAD_DIM)
    noise = jnp.clip(jax.random.normal(key, full_shape, jnp.float32), -6.0, 6.0)
    return noise.reshape(BATCH, VIEWS, SEQ_LEN, HEADS * HEAD_DIM).astype(jnp.bfloat16)


def draw_key_rows(key, part):
    key = jax.random.fold_in(key, 2)
    full_shape = (BATCH, VIEWS, SEQ_LEN, HEADS, HEAD_DIM)
    noise = jnp.clip(jax.random.normal(key, full_shape, jnp.float32), -6.0, 6.0)
    return noise.reshape(BATCH, VIEWS, SEQ_LEN, HEADS * HEAD_DIM).astype(jnp.bfloat16)


def draw_view_queries(key, part):
    key = jax.random.fold_in(key, 3)
    full_shape = (BATCH, VIEWS, SEQ_LEN, HEADS, HEAD_DIM)
    noise = jnp.clip(jax.random.normal(key, full_shape, jnp.float32), -6.0, 6.0)
    return noise.reshape(BATCH, VIEWS, SEQ_LEN, HEADS * HEAD_DIM).astype(jnp.bfloat16)


def block_levels(stream_key, extent, shards, smallest, largest):
    loudness, own = 1.0, jax.random.fold_in(stream_key, 6)
    for axis_at, parts in shards:
        steps = jnp.exp(jax.random.uniform(jax.random.fold_in(own, axis_at), (parts,), jnp.float32, smallest / len(shards), largest / len(shards)))
        loudness = loudness * jnp.repeat(steps, extent[axis_at] // parts).reshape([-1 if axis == axis_at else 1 for axis in range(len(extent))])
    return loudness


def bell_draw(rng, extent, spread, bound, cuts=(), kind=jnp.bfloat16):
    level = block_levels(rng, extent, cuts, -0.22, 0.18) if cuts else 1.0
    entries = jax.random.normal(rng, extent, jnp.float32) * spread * level
    return jnp.minimum(jnp.maximum(entries, -bound), bound).astype(kind)


def setup_inputs(seed: int = 0) -> dict:
    key_list = jax.random.split(jax.random.key(seed), 5)
    return {
        "queries": draw_queries(jax.random.fold_in(key_list[4], 71), 0),
        "key_rows": draw_key_rows(jax.random.fold_in(key_list[4], 71), 0),
        "value_rows": bell_draw(key_list[2], (BATCH, VIEWS, SEQ_LEN, D), 1.0, 6.0, ((1, 8), (2, 64))),
        "view_queries": draw_view_queries(jax.random.fold_in(key_list[4], 71), 0),
    }


def view_attention(triple):
    query_part, key_part, value_part = triple
    length = query_part.shape[0]
    block_rows = min(512, length)
    score_scale = HEAD_DIM ** -0.5
    key_full = key_part.astype(jnp.float32)
    value_full = value_part.astype(jnp.float32)

    def one_block(query_block):
        scores = jnp.einsum("qhe,khe->hqk", query_block.astype(jnp.float32), key_full) * score_scale
        scores = scores - jnp.max(scores, axis=-1, keepdims=True)
        expo = jnp.exp(scores)
        weights = (expo / jnp.sum(expo, axis=-1, keepdims=True)).astype(jnp.bfloat16)
        weights = lax.optimization_barrier(weights).astype(jnp.float32)
        result = jnp.einsum("hqk,khe->qhe", weights, value_full)
        return result.astype(jnp.bfloat16)

    blocks = query_part.reshape(length // block_rows, block_rows, HEADS, HEAD_DIM)
    return lax.map(one_block, blocks).reshape(length, HEADS, HEAD_DIM)


def across_views(triple):
    cross_query, key_part, output_part = triple
    score_scale = HEAD_DIM ** -0.5
    scores = jnp.einsum("vshe,wshe->shvw", cross_query.astype(jnp.float32), key_part.astype(jnp.float32)) * score_scale
    scores = scores - jnp.max(scores, axis=-1, keepdims=True)
    expo = jnp.exp(scores)
    weights = (expo / jnp.sum(expo, axis=-1, keepdims=True)).astype(jnp.bfloat16)
    weights = lax.optimization_barrier(weights).astype(jnp.float32)
    result = jnp.einsum("shvw,wshe->vshe", weights, output_part.astype(jnp.float32))
    return result.astype(jnp.bfloat16)


def reference(queries, key_rows, value_rows, view_queries):
    batch_size, view_count, length, model_width = queries.shape
    flat_shape = (batch_size * view_count, length, HEADS, HEAD_DIM)
    spatial = lax.map(view_attention, (queries.reshape(flat_shape), key_rows.reshape(flat_shape), value_rows.reshape(flat_shape)))
    spatial = spatial.reshape(batch_size, view_count, length, model_width)
    split_shape = (batch_size, view_count, length, HEADS, HEAD_DIM)
    joined = lax.map(across_views, (view_queries.reshape(split_shape), key_rows.reshape(split_shape), spatial.reshape(split_shape)))
    joined = joined.reshape(batch_size, view_count, length, model_width)
    return spatial, joined
```

```python
import jax
import jax.numpy as jnp
from jax import lax
from jax.experimental import pallas as pl
from jax.experimental.pallas import tpu as pltpu
from jax.sharding import PartitionSpec as P

MESH = pl.DeviceIdType.MESH
BF16, F32 = jnp.bfloat16, jnp.float32
BATCH, VIEWS, SEQ_LEN, D = 4, 8, 2048, 2048
TOKENS = 32
PAIR = 128
HALF = 64
GROUPS = D // PAIR
SHARE = SEQ_LEN // VIEWS
SCALE = 0.125 * 1.4426950408889634


def rows(start, size):
    return pl.ds(pl.multiple_of(start, TOKENS), size)


def low_lanes(count):
    return lax.broadcasted_iota(jnp.int32, (count, PAIR), 1) < HALF


def split_queries(block):
    low = low_lanes(block.shape[0])
    scaled = block.astype(F32) * SCALE
    first = scaled.astype(BF16).astype(F32)
    second = pltpu.roll(scaled - first, HALF, 1)
    return jnp.where(low, first, second).astype(BF16), jnp.where(low, second, first).astype(BF16)


def twin_keys(block):
    low = low_lanes(block.shape[0])
    plain = block.astype(F32)
    moved = pltpu.roll(plain, HALF, 1)
    return jnp.where(low, plain, moved).astype(BF16), jnp.where(low, moved, plain).astype(BF16)


def values_and_ones(block):
    low = low_lanes(block.shape[0])
    plain = block.astype(F32)
    return jnp.where(low, plain, 1.0).astype(BF16), jnp.where(low, 1.0, plain).astype(BF16)


def weigh(query, key, value, mask=None):
    scores = lax.dot_general(query, key, (((1,), (1,)), ((), ())), preferred_element_type=F32)
    if mask is not None:
        scores = jnp.where(mask, scores, -1e30)
    scores = scores - jnp.max(scores, axis=1, keepdims=True)
    return jnp.dot(jnp.exp2(scores).astype(BF16), value, preferred_element_type=F32)


def finish(first, second):
    low = low_lanes(first.shape[0])
    total = pltpu.roll(jnp.where(low, second, first), HALF, 1)
    return (jnp.where(low, first, second) / total).astype(BF16)


def kernel(
    queries, key_rows, value_rows, view_queries, spatial, joined,
    k_in, v_in, q_in, w_in, k_a, k_b, v_a, v_b, o_out, k_views, o_views, j_out,
    in_sent, in_here, k_sent, k_here, o_sent, o_here, home_sent, home_here,
):
    view, seq = lax.axis_index("view"), lax.axis_index("seq")
    z_hi, y = view // 4, view % 4
    z_lo, x, core = seq // 8, (seq // 2) % 4, seq % 2
    z = z_hi * 8 + z_lo
    my_pair = z * 4 + x
    my_view = core * 4 + y
    b, g = my_pair // GROUPS, my_pair % GROUPS
    view_stays = z_hi == core
    share_stays = z_lo == my_view

    def at(z, y, x, core):
        return ((z // 8) * 4 + y, (z % 8) * 8 + x * 2 + core)

    def place(ref, b, g):
        return ref.at[b, 0, :, pl.ds(pl.multiple_of(g * PAIR, PAIR), PAIR)]

    def send(src, dst, sent, here, device, stays):
        @pl.when(jnp.logical_not(stays))
        def _():
            pltpu.make_async_remote_copy(src, dst, sent, here, device_id=device, device_id_type=MESH).start()

        @pl.when(stays)
        def _():
            pltpu.make_async_copy(src, dst, here).start()

    def wait(ref, sem):
        pltpu.make_async_copy(ref, ref, sem).wait()

    def wait_sent(sem, stays):
        @pl.when(stays)
        def _():
            wait(q_in.at[pl.ds(0, SEQ_LEN - TOKENS)], sem)

        @pl.when(jnp.logical_not(stays))
        def _():
            wait(q_in, sem)

    barrier = pltpu.get_barrier_semaphore()

    def greet(device, stays):
        @pl.when(jnp.logical_not(stays))
        def _():
            pl.semaphore_signal(barrier, inc=1, device_id=device, device_id_type=MESH)

    @pl.loop(0, 64)
    def _(i):
        c2, x2, z2 = i % 2, (i // 2) % 4, i // 8
        greet(at(core * 8 + z2, y, x2, c2), view_stays & (z2 == z_lo) & (x2 == x) & (c2 == core))
        greet(at((i // 32) * 8 + my_view, (i // 8) % 4, x2, c2), share_stays & (i // 8 == view) & (x2 == x) & (c2 == core))

    @pl.loop(1, VIEWS)
    def _(i):
        other = (my_view + i) % VIEWS
        greet(at(z, other % 4, x, other // 4), False)

    expected = 2 * 64 + VIEWS - 1 - view_stays.astype(jnp.int32) - share_stays.astype(jnp.int32)
    pl.semaphore_wait(barrier, expected)

    for which, (array, buffer) in enumerate(((key_rows, k_in), (value_rows, v_in), (queries, q_in))):

        @pl.loop(0, 64)
        def _(i):
            z2, x2 = (z + i // 4) % 16, (x + i) % 4
            pair = z2 * 4 + x2
            send(
                place(array, pair // GROUPS, pair % GROUPS),
                buffer.at[rows(seq * TOKENS, TOKENS)],
                in_sent.at[which],
                in_here.at[which],
                at(z2, y, x2, z_hi),
                view_stays & (i == 0),
            )

    @pl.loop(0, 64)
    def _(i):
        z2, x2 = (z + i // 4) % 16, (x + i) % 4
        pair = z2 * 4 + x2
        send(
            place(view_queries, pair // GROUPS, pair % GROUPS),
            w_in.at[view, rows((seq % 8) * TOKENS, TOKENS)],
            in_sent.at[3],
            in_here.at[3],
            at(z2, z_lo % 4, x2, z_lo // 4),
            share_stays & (i == 0),
        )

    wait(k_in, in_here.at[0])

    @pl.loop(0, VIEWS)
    def _(i):
        other = (my_view + i) % VIEWS
        send(
            k_in.at[rows(other * SHARE, SHARE)],
            k_views.at[my_view],
            k_sent,
            k_here,
            at(z, other % 4, x, other // 4),
            i == 0,
        )

    k_a[...], k_b[...] = twin_keys(k_in[...])
    wait(v_in, in_here.at[1])
    v_a[...], v_b[...] = values_and_ones(v_in[...])
    wait(q_in, in_here.at[2])

    @pl.loop(0, VIEWS)
    def _(i):
        part = (z_lo + i) % VIEWS
        here = rows(part * SHARE, SHARE)
        q_a, q_b = split_queries(q_in[here])
        o_out[here] = finish(weigh(q_a, k_a[...], v_a[...]), weigh(q_b, k_b[...], v_b[...]))
        send(
            o_out.at[here],
            o_views.at[my_view],
            o_sent,
            o_here,
            at(z, part % 4, x, part // 4),
            part == my_view,
        )

        @pl.loop(0, 8)
        def _(n):
            x2, c2 = (x + n // 2) % 4, n % 2
            send(
                o_out.at[rows(part * SHARE + (x2 * 2 + c2) * TOKENS, TOKENS)],
                place(spatial, b, g),
                home_sent.at[0],
                home_here.at[0],
                at(core * 8 + part, y, x2, c2),
                view_stays & (part == z_lo) & (x2 == x) & (c2 == core),
            )

    wait(k_views, k_here)
    wait(w_in, in_here.at[3])
    wait(o_views, o_here)
    count = VIEWS * TOKENS
    same = (
        lax.broadcasted_iota(jnp.int32, (count, count), 0) % TOKENS
        == lax.broadcasted_iota(jnp.int32, (count, count), 1) % TOKENS
    )

    @pl.loop(0, 8)
    def _(i):
        x2, c2 = (x + i // 2) % 4, i % 2
        here = rows((x2 * 2 + c2) * TOKENS, TOKENS)
        q_1, q_2 = split_queries(w_in[:, here].reshape(count, PAIR))
        k_1, k_2 = twin_keys(k_views[:, here].reshape(count, PAIR))
        v_1, v_2 = values_and_ones(o_views[:, here].reshape(count, PAIR))
        result = finish(weigh(q_1, k_1, v_1, same), weigh(q_2, k_2, v_2, same))
        j_out[:, here] = result.reshape(VIEWS, TOKENS, PAIR)

        @pl.loop(0, VIEWS)
        def _(n):
            v2 = (view + n) % VIEWS
            send(
                j_out.at[v2, here],
                place(joined, b, g),
                home_sent.at[1],
                home_here.at[1],
                at((v2 // 4) * 8 + my_view, v2 % 4, x2, c2),
                share_stays & (n == 0) & (i // 2 == 0) & (c2 == core),
            )

    for which, stays in enumerate((view_stays, view_stays, view_stays, share_stays)):
        wait_sent(in_sent.at[which], stays)
    wait(q_in.at[pl.ds(0, SEQ_LEN - SHARE)], k_sent)
    wait(q_in.at[pl.ds(0, SEQ_LEN - SHARE)], o_sent)
    wait_sent(home_sent.at[0], view_stays)
    wait_sent(home_sent.at[1], share_stays)
    wait(spatial, home_here.at[0])
    wait(joined, home_here.at[1])


def local(queries, key_rows, value_rows, view_queries):
    whole, shares = (SEQ_LEN, PAIR), (VIEWS, SHARE, PAIR)
    return pl.pallas_call(
        kernel,
        out_shape=[jax.ShapeDtypeStruct(queries.shape, BF16)] * 2,
        in_specs=[pl.BlockSpec(memory_space=pl.ANY)] * 4,
        out_specs=[pl.BlockSpec(memory_space=pl.ANY)] * 2,
        scratch_shapes=[
            *[pltpu.VMEM(whole, BF16)] * 3,
            pltpu.VMEM(shares, BF16),
            *[pltpu.VMEM(whole, BF16)] * 5,
            *[pltpu.VMEM(shares, BF16)] * 3,
            pltpu.SemaphoreType.DMA((4,)),
            pltpu.SemaphoreType.DMA((4,)),
            *[pltpu.SemaphoreType.DMA] * 4,
            pltpu.SemaphoreType.DMA((2,)),
            pltpu.SemaphoreType.DMA((2,)),
        ],
        compiler_params=pltpu.CompilerParams(
            collective_id=0, has_side_effects=True, vmem_limit_bytes=48 << 20
        ),
        cost_estimate=pl.CostEstimate(flops=1 << 32, bytes_accessed=1 << 22, transcendentals=1 << 23),
    )(queries, key_rows, value_rows, view_queries)


def solution(mesh):
    placed = P(None, "view", "seq", None)
    return jax.shard_map(
        local, mesh=mesh, in_specs=(placed,) * 4, out_specs=(placed, placed), check_vma=False
    )
```

```python
import jax
import jax.numpy as jnp
from jax import lax
from jax.experimental import pallas as pl
from jax.experimental.pallas import tpu as pltpu
from jax.sharding import PartitionSpec as P

MESH = pl.DeviceIdType.MESH
BF16, F32 = jnp.bfloat16, jnp.float32
BATCH, VIEWS, SEQ_LEN, D = 4, 8, 2048, 2048
TOKENS = 32
PAIR = 128
HALF = 64
GROUPS = D // PAIR
SHARE = SEQ_LEN // VIEWS
SCALE = 0.125 * 1.4426950408889634


def rows(start, size):
    return pl.ds(pl.multiple_of(start, TOKENS), size)


def low_lanes(count):
    return lax.broadcasted_iota(jnp.int32, (count, PAIR), 1) < HALF


def split_queries(block):
    low = low_lanes(block.shape[0])
    scaled = block.astype(F32) * SCALE
    first = scaled.astype(BF16).astype(F32)
    second = pltpu.roll(scaled - first, HALF, 1)
    return jnp.where(low, first, second).astype(BF16), jnp.where(low, second, first).astype(BF16)


def twin_keys(block):
    low = low_lanes(block.shape[0])
    plain = block.astype(F32)
    moved = pltpu.roll(plain, HALF, 1)
    return jnp.where(low, plain, moved).astype(BF16), jnp.where(low, moved, plain).astype(BF16)


def values_and_ones(block):
    low = low_lanes(block.shape[0])
    plain = block.astype(F32)
    return jnp.where(low, plain, 1.0).astype(BF16), jnp.where(low, 1.0, plain).astype(BF16)


def weigh(query, key, value, mask=None):
    scores = lax.dot_general(query, key, (((1,), (1,)), ((), ())), preferred_element_type=F32)
    if mask is not None:
        scores = jnp.where(mask, scores, -1e30)
    scores = scores - jnp.max(scores, axis=1, keepdims=True)
    return jnp.dot(jnp.exp2(scores).astype(BF16), value, preferred_element_type=F32)


def finish(first, second):
    low = low_lanes(first.shape[0])
    total = pltpu.roll(jnp.where(low, second, first), HALF, 1)
    return (jnp.where(low, first, second) / total).astype(BF16)


def kernel(
    queries, key_rows, value_rows, view_queries, spatial, joined,
    k_in, v_in, q_in, w_in, k_a, k_b, v_a, v_b, o_out, k_views, o_views, j_out,
    in_sent, in_here, q_here, leave, k_sent, k_here, o_sent, o_here, home_sent, home_here,
):
    view, seq = lax.axis_index("view"), lax.axis_index("seq")
    z_hi, y = view // 4, view % 4
    z_lo, x, core = seq // 8, (seq // 2) % 4, seq % 2
    z = z_hi * 8 + z_lo
    my_pair = z * 4 + x
    my_view = core * 4 + y
    b, g = my_pair // GROUPS, my_pair % GROUPS
    view_stays = z_hi == core
    my_share = (y % 2) + 2 * core + 4 * (y // 2)
    turn = z_lo + x + 4 * core
    share_stays = (turn + x) % VIEWS == my_share

    def at(z, y, x, core):
        return ((z // 8) * 4 + y, (z % 8) * 8 + x * 2 + core)

    def combiner(share):
        return (share % 2) + 2 * (share // 4), (share // 2) % 2

    def home_of(share, part):
        turn = (share - x - part + 2 * VIEWS) % VIEWS
        return turn % 4, turn // 4

    def place(ref, b, g):
        return ref.at[b, 0, :, pl.ds(pl.multiple_of(g * PAIR, PAIR), PAIR)]

    def send(src, dst, sent, here, device, stays):
        @pl.when(jnp.logical_not(stays))
        def _():
            pltpu.make_async_remote_copy(src, dst, sent, here, device_id=device, device_id_type=MESH).start()

        @pl.when(stays)
        def _():
            pltpu.make_async_copy(src, dst, here).start()

    def wait(ref, sem):
        pltpu.make_async_copy(ref, ref, sem).wait()

    def wait_sent(sem, stays):
        @pl.when(stays)
        def _():
            wait(q_in.at[pl.ds(0, SEQ_LEN - TOKENS)], sem)

        @pl.when(jnp.logical_not(stays))
        def _():
            wait(q_in, sem)

    barrier = pltpu.get_barrier_semaphore()
    first = view_stays.astype(jnp.int32)

    @pl.loop(first, 64)
    def _(i):
        pl.semaphore_signal(barrier, inc=1, device_id=(my_view, (seq + i) % 64), device_id_type=MESH)

    for i in range(1, VIEWS):
        other = (my_view + i) % VIEWS
        pl.semaphore_signal(barrier, inc=1, device_id=at(z, other % 4, x, other // 4), device_id_type=MESH)
    pl.semaphore_wait(barrier, 64 + VIEWS - 1 - first)

    def scatter(array, step, target):
        for dx in range(4):
            z2, x2 = (z + step) % 16, (x + dx) % 4
            pair = z2 * 4 + x2
            target(place(array, pair // GROUPS, pair % GROUPS), z2, x2, (step == 0) & (dx == 0))

    for which, (array, buffer) in enumerate(((key_rows, k_in), (value_rows, v_in), (queries, q_in))):

        @pl.loop(0, 16)
        def _(step):
            def target(src, z2, x2, own):
                if which == 2:
                    row = seq * TOKENS
                else:
                    row = (turn + x2) % VIEWS * SHARE + z_lo * TOKENS
                dst = buffer.at[rows(row, TOKENS)]
                here = q_here.at[z_lo] if which == 2 else in_here.at[which]
                send(src, dst, in_sent.at[which], here, at(z2, y, x2, z_hi), view_stays & own)

            scatter(array, step, target)

    wait(k_in, in_here.at[0])

    @pl.loop(first, 64)
    def _(i):
        pl.semaphore_signal(leave, inc=1, device_id=(my_view, (seq + i) % 64), device_id_type=MESH)

    @pl.loop(0, VIEWS)
    def _(i):
        share = (my_share + i) % VIEWS
        y2, c2 = combiner(share)
        send(k_in.at[rows(share * SHARE, SHARE)], k_views.at[my_view], k_sent, k_here, at(z, y2, x, c2), i == 0)

    k_a[...], k_b[...] = twin_keys(k_in[...])
    pl.semaphore_wait(leave, 64 - first)
    wait(v_in, in_here.at[1])
    v_a[...], v_b[...] = values_and_ones(v_in[...])

    @pl.loop(0, VIEWS)
    def _(i):
        part = (jnp.where(view_stays, z_lo, 7) + VIEWS - i) % VIEWS
        here = rows(part * SHARE, SHARE)
        wait(q_in.at[here], q_here.at[part])
        q_a, q_b = split_queries(q_in[here])
        o_out[here] = finish(weigh(q_a, k_a[...], v_a[...]), weigh(q_b, k_b[...], v_b[...]))
        for n in range(8):
            share = (my_share + n) % VIEWS
            y2, c2 = combiner(share)
            x2, from2 = home_of(share, part)
            send(
                o_out.at[rows(part * SHARE + (x2 * 2 + from2) * TOKENS, TOKENS)],
                o_views.at[my_view, rows(part * TOKENS, TOKENS)],
                o_sent,
                o_here,
                at(z, y2, x, c2),
                n == 0,
            )

        def target(src, z2, x2, own):
            y2, c2 = combiner((turn + x2) % VIEWS)
            dst = w_in.at[view, rows(z_lo * TOKENS, TOKENS)]
            send(src, dst, in_sent.at[3], in_here.at[3], at(z2, y2, x2, c2), share_stays & own)

        scatter(view_queries, 2 * i, target)
        scatter(view_queries, 2 * i + 1, target)

    @pl.loop(0, VIEWS)
    def _(i):
        part = (jnp.where(view_stays, z_lo, 7) + VIEWS - i) % VIEWS
        for n in range(8):
            x2, c2 = (x + n // 2) % 4, n % 2
            send(
                o_out.at[rows(part * SHARE + (x2 * 2 + c2) * TOKENS, TOKENS)],
                place(spatial, b, g),
                home_sent.at[0],
                home_here.at[0],
                at(core * 8 + part, y, x2, c2),
                view_stays & (part == z_lo) & (x2 == x) & (c2 == core),
            )

    wait(k_views, k_here)
    wait(w_in, in_here.at[3])
    wait(o_views, o_here)
    count = VIEWS * TOKENS
    same = (
        lax.broadcasted_iota(jnp.int32, (count, count), 0) % TOKENS
        == lax.broadcasted_iota(jnp.int32, (count, count), 1) % TOKENS
    )

    @pl.loop(0, VIEWS)
    def _(i):
        part = (z_lo + i) % VIEWS
        x2, c2 = home_of(my_share, part)
        here = rows(part * TOKENS, TOKENS)
        q_1, q_2 = split_queries(w_in[:, here].reshape(count, PAIR))
        k_1, k_2 = twin_keys(k_views[:, here].reshape(count, PAIR))
        v_1, v_2 = values_and_ones(o_views[:, here].reshape(count, PAIR))
        result = finish(weigh(q_1, k_1, v_1, same), weigh(q_2, k_2, v_2, same))
        j_out[:, here] = result.reshape(VIEWS, TOKENS, PAIR)

        for n in range(VIEWS):
            v2 = (view + n) % VIEWS
            send(
                j_out.at[v2, here],
                place(joined, b, g),
                home_sent.at[1],
                home_here.at[1],
                at((v2 // 4) * 8 + part, v2 % 4, x2, c2),
                share_stays & (n == 0) & (i == 0),
            )

    for which, stays in enumerate((view_stays, view_stays, view_stays, share_stays)):
        wait_sent(in_sent.at[which], stays)
    wait(q_in.at[pl.ds(0, SEQ_LEN - SHARE)], k_sent)
    wait(q_in.at[pl.ds(0, SEQ_LEN - SHARE)], o_sent)
    wait_sent(home_sent.at[0], view_stays)
    wait_sent(home_sent.at[1], share_stays)
    wait(spatial, home_here.at[0])
    wait(joined, home_here.at[1])


def local(queries, key_rows, value_rows, view_queries):
    whole, shares = (SEQ_LEN, PAIR), (VIEWS, SHARE, PAIR)
    return pl.pallas_call(
        kernel,
        out_shape=[jax.ShapeDtypeStruct(queries.shape, BF16)] * 2,
        in_specs=[pl.BlockSpec(memory_space=pl.ANY)] * 4,
        out_specs=[pl.BlockSpec(memory_space=pl.ANY)] * 2,
        scratch_shapes=[
            *[pltpu.VMEM(whole, BF16)] * 3,
            pltpu.VMEM(shares, BF16),
            *[pltpu.VMEM(whole, BF16)] * 5,
            *[pltpu.VMEM(shares, BF16)] * 3,
            pltpu.SemaphoreType.DMA((4,)),
            pltpu.SemaphoreType.DMA((4,)),
            pltpu.SemaphoreType.DMA((VIEWS,)),
            pltpu.SemaphoreType.REGULAR,
            *[pltpu.SemaphoreType.DMA] * 4,
            pltpu.SemaphoreType.DMA((2,)),
            pltpu.SemaphoreType.DMA((2,)),
        ],
        compiler_params=pltpu.CompilerParams(
            collective_id=0, has_side_effects=True, vmem_limit_bytes=60 << 20
        ),
        cost_estimate=pl.CostEstimate(flops=1 << 32, bytes_accessed=1 << 22, transcendentals=1 << 23),
    )(queries, key_rows, value_rows, view_queries)


def solution(mesh):
    placed = P(None, "view", "seq", None)
    return jax.shard_map(
        local, mesh=mesh, in_specs=(placed,) * 4, out_specs=(placed, placed), check_vma=False
    )
```

```python
import jax
import jax.numpy as jnp
from jax import lax
from jax.experimental import pallas as pl
from jax.experimental.pallas import tpu as pltpu
from jax.sharding import PartitionSpec as P

MESH = pl.DeviceIdType.MESH
BF16, F32 = jnp.bfloat16, jnp.float32
BATCH, VIEWS, SEQ_LEN, D = 4, 8, 2048, 2048
TOKENS = 32
PAIR = 128
HALF = 64
GROUPS = D // PAIR
SHARE = SEQ_LEN // VIEWS
SCALE = 0.125 * 1.4426950408889634


def rows(start, size):
    return pl.ds(pl.multiple_of(start, TOKENS), size)


def low_lanes(count):
    return lax.broadcasted_iota(jnp.int32, (count, PAIR), 1) < HALF


def split_queries(block):
    low = low_lanes(block.shape[0])
    scaled = block.astype(F32) * SCALE
    first = scaled.astype(BF16).astype(F32)
    second = pltpu.roll(scaled - first, HALF, 1)
    return jnp.where(low, first, second).astype(BF16), jnp.where(low, second, first).astype(BF16)


def twin_keys(block):
    low = low_lanes(block.shape[0])
    plain = block.astype(F32)
    moved = pltpu.roll(plain, HALF, 1)
    return jnp.where(low, plain, moved).astype(BF16), jnp.where(low, moved, plain).astype(BF16)


def values_and_ones(block):
    low = low_lanes(block.shape[0])
    plain = block.astype(F32)
    return jnp.where(low, plain, 1.0).astype(BF16), jnp.where(low, 1.0, plain).astype(BF16)


def weigh(query, key, value, mask=None):
    scores = lax.dot_general(query, key, (((1,), (1,)), ((), ())), preferred_element_type=F32)
    if mask is not None:
        scores = jnp.where(mask, scores, -1e30)
    scores = scores - jnp.max(scores, axis=1, keepdims=True)
    return jnp.dot(jnp.exp2(scores).astype(BF16), value, preferred_element_type=F32)


def finish(first, second):
    low = low_lanes(first.shape[0])
    total = pltpu.roll(jnp.where(low, second, first), HALF, 1)
    return (jnp.where(low, first, second) / total).astype(BF16)


def kernel(
    queries, key_rows, value_rows, view_queries, spatial, joined,
    k_in, v_in, q_in, w_in, k_a, k_b, v_a, v_b, o_out, k_views, o_views, j_out,
    in_sent, in_here, q_here, leave, k_sent, k_here, o_sent, o_here, home_sent, home_here,
):
    view, seq = lax.axis_index("view"), lax.axis_index("seq")
    z_hi, y = view // 4, view % 4
    z_lo, x, core = seq // 8, (seq // 2) % 4, seq % 2
    z = z_hi * 8 + z_lo
    my_pair = z * 4 + x
    my_view = core * 4 + y
    b, g = my_pair // GROUPS, my_pair % GROUPS
    view_stays = z_hi == core
    my_share = (y % 2) + 2 * core + 4 * (y // 2)
    turn = z_lo + x + 4 * core
    share_stays = (turn + x) % VIEWS == my_share

    def at(z, y, x, core):
        return ((z // 8) * 4 + y, (z % 8) * 8 + x * 2 + core)

    def combiner(share):
        return (share % 2) + 2 * (share // 4), (share // 2) % 2

    def home_of(share, part):
        turn = (share - x - part + 2 * VIEWS) % VIEWS
        return turn % 4, turn // 4

    def place(ref, b, g):
        return ref.at[b, 0, :, pl.ds(pl.multiple_of(g * PAIR, PAIR), PAIR)]

    def send(src, dst, sent, here, device, stays):
        if stays is False:
            pltpu.make_async_remote_copy(src, dst, sent, here, device_id=device, device_id_type=MESH).start()
            return

        if stays is True:
            pltpu.make_async_copy(src, dst, here).start()
            return

        @pl.when(jnp.logical_not(stays))
        def _():
            pltpu.make_async_remote_copy(src, dst, sent, here, device_id=device, device_id_type=MESH).start()

        @pl.when(stays)
        def _():
            pltpu.make_async_copy(src, dst, here).start()

    def wait(ref, sem):
        pltpu.make_async_copy(ref, ref, sem).wait()

    def wait_sent(sem, stays):
        @pl.when(stays)
        def _():
            wait(q_in.at[pl.ds(0, SEQ_LEN - TOKENS)], sem)

        @pl.when(jnp.logical_not(stays))
        def _():
            wait(q_in, sem)

    barrier = pltpu.get_barrier_semaphore()
    first = view_stays.astype(jnp.int32)

    def tell_tokens(sem):
        @pl.when(jnp.logical_not(view_stays))
        def _():
            pl.semaphore_signal(sem, inc=1, device_id=(my_view, seq), device_id_type=MESH)

        @pl.loop(1, 64, unroll=9)
        def _(i):
            pl.semaphore_signal(sem, inc=1, device_id=(my_view, lax.rem(seq + i, 64)), device_id_type=MESH)

    tell_tokens(barrier)

    for i in range(1, VIEWS):
        other = (my_view + i) % VIEWS
        pl.semaphore_signal(barrier, inc=1, device_id=at(z, other % 4, x, other // 4), device_id_type=MESH)
    pl.semaphore_wait(barrier, 64 + VIEWS - 1 - first)

    def scatter(array, step, target):
        for far in (0, 8):
            z2 = (z + step + far) % 16
            for dx in range(4):
                x2 = (x + dx) % 4
                pair = z2 * 4 + x2
                own = step == 0 if (far, dx) == (0, 0) else False
                target(place(array, pair // GROUPS, pair % GROUPS), z2, x2, own)

    for which, (array, buffer) in enumerate(((key_rows, k_in), (value_rows, v_in), (queries, q_in))):

        @pl.loop(0, 8)
        def _(step):
            def target(src, z2, x2, own):
                if which == 2:
                    row = seq * TOKENS
                else:
                    row = (turn + x2) % VIEWS * SHARE + z_lo * TOKENS
                dst = buffer.at[rows(row, TOKENS)]
                here = q_here.at[z_lo] if which == 2 else in_here.at[which]
                send(src, dst, in_sent.at[which], here, at(z2, y, x2, z_hi), False if own is False else view_stays & own)

            scatter(array, step, target)

    wait(k_in, in_here.at[0])

    tell_tokens(leave)

    @pl.loop(0, VIEWS)
    def _(i):
        share = (my_share + i) % VIEWS
        y2, c2 = combiner(share)
        send(k_in.at[rows(share * SHARE, SHARE)], k_views.at[my_view], k_sent, k_here, at(z, y2, x, c2), i == 0)

    k_a[...], k_b[...] = twin_keys(k_in[...])
    pl.semaphore_wait(leave, 64 - first)

    @pl.loop(0, VIEWS)
    def _(i):
        def target(src, z2, x2, own):
            y2, c2 = combiner((turn + x2) % VIEWS)
            dst = w_in.at[view, rows(z_lo * TOKENS, TOKENS)]
            send(src, dst, in_sent.at[3], in_here.at[3], at(z2, y2, x2, c2), False if own is False else share_stays & own)

        scatter(view_queries, i, target)

    wait(v_in, in_here.at[1])
    v_a[...], v_b[...] = values_and_ones(v_in[...])

    @pl.loop(0, VIEWS)
    def _(i):
        part = (z_lo + VIEWS - i) % VIEWS
        here = rows(part * SHARE, SHARE)
        wait(q_in.at[here], q_here.at[part])
        q_a, q_b = split_queries(q_in[here])
        o_out[here] = finish(weigh(q_a, k_a[...], v_a[...]), weigh(q_b, k_b[...], v_b[...]))
        for n in range(8):
            share = (my_share + n) % VIEWS
            y2, c2 = combiner(share)
            x2, from2 = home_of(share, part)
            send(
                o_out.at[rows(part * SHARE + (x2 * 2 + from2) * TOKENS, TOKENS)],
                o_views.at[my_view, rows(part * TOKENS, TOKENS)],
                o_sent,
                o_here,
                at(z, y2, x, c2),
                n == 0,
            )


    @pl.loop(0, VIEWS)
    def _(i):
        part = (z_lo + VIEWS - i) % VIEWS
        for n in range(8):
            x2, c2 = (x + n // 2) % 4, (core + n) % 2
            send(
                o_out.at[rows(part * SHARE + (x2 * 2 + c2) * TOKENS, TOKENS)],
                place(spatial, b, g),
                home_sent.at[0],
                home_here.at[0],
                at(core * 8 + part, y, x2, c2),
                view_stays & (i == 0) if n == 0 else False,
            )

    wait(k_views, k_here)
    wait(w_in, in_here.at[3])
    wait(o_views, o_here)
    count = VIEWS * TOKENS
    same = (
        lax.broadcasted_iota(jnp.int32, (count, count), 0) % TOKENS
        == lax.broadcasted_iota(jnp.int32, (count, count), 1) % TOKENS
    )

    @pl.loop(0, VIEWS)
    def _(i):
        part = (z_lo + VIEWS - i) % VIEWS
        x2, c2 = home_of(my_share, part)
        here = rows(part * TOKENS, TOKENS)
        q_1, q_2 = split_queries(w_in[:, here].reshape(count, PAIR))
        k_1, k_2 = twin_keys(k_views[:, here].reshape(count, PAIR))
        v_1, v_2 = values_and_ones(o_views[:, here].reshape(count, PAIR))
        result = finish(weigh(q_1, k_1, v_1, same), weigh(q_2, k_2, v_2, same))
        j_out[:, here] = result.reshape(VIEWS, TOKENS, PAIR)

        for n in range(VIEWS):
            v2 = (view + n) % VIEWS
            send(
                j_out.at[v2, here],
                place(joined, b, g),
                home_sent.at[1],
                home_here.at[1],
                at((v2 // 4) * 8 + part, v2 % 4, x2, c2),
                share_stays & (i == 0) if n == 0 else False,
            )

    for which, stays in enumerate((view_stays, view_stays, view_stays, share_stays)):
        wait_sent(in_sent.at[which], stays)
    wait(q_in.at[pl.ds(0, SEQ_LEN - SHARE)], k_sent)
    wait(q_in.at[pl.ds(0, SEQ_LEN - SHARE)], o_sent)
    wait_sent(home_sent.at[0], view_stays)
    wait_sent(home_sent.at[1], share_stays)
    wait(spatial, home_here.at[0])
    wait(joined, home_here.at[1])


def local(queries, key_rows, value_rows, view_queries):
    whole, shares = (SEQ_LEN, PAIR), (VIEWS, SHARE, PAIR)
    return pl.pallas_call(
        kernel,
        out_shape=[jax.ShapeDtypeStruct(queries.shape, BF16)] * 2,
        in_specs=[pl.BlockSpec(memory_space=pl.ANY)] * 4,
        out_specs=[pl.BlockSpec(memory_space=pl.ANY)] * 2,
        scratch_shapes=[
            *[pltpu.VMEM(whole, BF16)] * 3,
            pltpu.VMEM(shares, BF16),
            *[pltpu.VMEM(whole, BF16)] * 5,
            *[pltpu.VMEM(shares, BF16)] * 3,
            pltpu.SemaphoreType.DMA((4,)),
            pltpu.SemaphoreType.DMA((4,)),
            pltpu.SemaphoreType.DMA((VIEWS,)),
            pltpu.SemaphoreType.REGULAR,
            *[pltpu.SemaphoreType.DMA] * 4,
            pltpu.SemaphoreType.DMA((2,)),
            pltpu.SemaphoreType.DMA((2,)),
        ],
        compiler_params=pltpu.CompilerParams(
            collective_id=0, has_side_effects=True, vmem_limit_bytes=105 << 19
        ),
        cost_estimate=pl.CostEstimate(flops=1 << 32, bytes_accessed=1 << 22, transcendentals=1 << 23),
    )(queries, key_rows, value_rows, view_queries)


def solution(mesh):
    placed = P(None, "view", "seq", None)
    return jax.shard_map(
        local, mesh=mesh, in_specs=(placed,) * 4, out_specs=(placed, placed), check_vma=False
    )
```

```python
import jax
import jax.numpy as jnp
from jax import lax
from jax.experimental import pallas as pl
from jax.experimental.pallas import tpu as pltpu
from jax.sharding import PartitionSpec as P

MESH = pl.DeviceIdType.MESH
BF16, F32 = jnp.bfloat16, jnp.float32
BATCH, VIEWS, SEQ_LEN, D = 4, 8, 2048, 2048
TOKENS = 32
PAIR = 128
HALF = 64
GROUPS = D // PAIR
SHARE = SEQ_LEN // VIEWS
LATER = 6
SCALE = 0.125 * 1.4426950408889634


def rows(start, size):
    return pl.ds(pl.multiple_of(start, TOKENS), size)


def low_lanes(count):
    return lax.broadcasted_iota(jnp.int32, (count, PAIR), 1) < HALF


def split_queries(block):
    low = low_lanes(block.shape[0])
    scaled = block.astype(F32) * SCALE
    first = scaled.astype(BF16).astype(F32)
    second = pltpu.roll(scaled - first, HALF, 1)
    return jnp.where(low, first, second).astype(BF16), jnp.where(low, second, first).astype(BF16)


def twin_keys(block):
    low = low_lanes(block.shape[0])
    plain = block.astype(F32)
    moved = pltpu.roll(plain, HALF, 1)
    return jnp.where(low, plain, moved).astype(BF16), jnp.where(low, moved, plain).astype(BF16)


def values_and_ones(block):
    low = low_lanes(block.shape[0])
    plain = block.astype(F32)
    return jnp.where(low, plain, 1.0).astype(BF16), jnp.where(low, 1.0, plain).astype(BF16)


def weigh(query, key, value, mask=None):
    scores = lax.dot_general(query, key, (((1,), (1,)), ((), ())), preferred_element_type=F32)
    if mask is not None:
        scores = jnp.where(mask, scores, -1e30)
    scores = scores - jnp.max(scores, axis=1, keepdims=True)
    return jnp.dot(jnp.exp2(scores).astype(BF16), value, preferred_element_type=F32)


def finish(first, second):
    low = low_lanes(first.shape[0])
    total = pltpu.roll(jnp.where(low, second, first), HALF, 1)
    return (jnp.where(low, first, second) / total).astype(BF16)


def kernel(
    queries, key_rows, value_rows, view_queries, spatial, joined,
    k_in, v_in, q_in, w_in, k_a, k_b, v_a, v_b, o_out, k_views, o_views, j_out,
    in_sent, in_here, q_here, leave, k_sent, k_here, o_sent, o_here, home_sent, home_here,
):
    view, seq = lax.axis_index("view"), lax.axis_index("seq")
    z_hi, y = view // 4, view % 4
    z_lo, x, core = seq // 8, (seq // 2) % 4, seq % 2
    z = z_hi * 8 + z_lo
    my_pair = z * 4 + x
    my_view = core * 4 + y
    b, g = my_pair // GROUPS, my_pair % GROUPS
    view_stays = z_hi == core
    my_share = (y % 2) + 2 * core + 4 * (y // 2)
    turn = z_lo + x + 4 * core
    share_stays = (turn + x) % VIEWS == my_share

    def at(z, y, x, core):
        return ((z // 8) * 4 + y, (z % 8) * 8 + x * 2 + core)

    def combiner(share):
        return (share % 2) + 2 * (share // 4), (share // 2) % 2

    def home_of(share, part):
        turn = (share - x - part + 2 * VIEWS) % VIEWS
        return turn % 4, turn // 4

    def place(ref, b, g):
        return ref.at[b, 0, :, pl.ds(pl.multiple_of(g * PAIR, PAIR), PAIR)]

    def send(src, dst, sent, here, device, stays):
        if stays is False:
            pltpu.make_async_remote_copy(src, dst, sent, here, device_id=device, device_id_type=MESH).start()
            return

        if stays is True:
            pltpu.make_async_copy(src, dst, here).start()
            return

        @pl.when(jnp.logical_not(stays))
        def _():
            pltpu.make_async_remote_copy(src, dst, sent, here, device_id=device, device_id_type=MESH).start()

        @pl.when(stays)
        def _():
            pltpu.make_async_copy(src, dst, here).start()

    def wait(ref, sem):
        pltpu.make_async_copy(ref, ref, sem).wait()

    def wait_sent(sem, stays):
        @pl.when(stays)
        def _():
            wait(q_in.at[pl.ds(0, SEQ_LEN - TOKENS)], sem)

        @pl.when(jnp.logical_not(stays))
        def _():
            wait(q_in, sem)

    barrier = pltpu.get_barrier_semaphore()
    first = view_stays.astype(jnp.int32)

    def tell_tokens(sem):
        @pl.when(jnp.logical_not(view_stays))
        def _():
            pl.semaphore_signal(sem, inc=1, device_id=(my_view, seq), device_id_type=MESH)

        @pl.loop(1, 64, unroll=9)
        def _(i):
            pl.semaphore_signal(sem, inc=1, device_id=(my_view, lax.rem(seq + i, 64)), device_id_type=MESH)

    tell_tokens(barrier)

    for i in range(1, VIEWS):
        other = (my_view + i) % VIEWS
        pl.semaphore_signal(barrier, inc=1, device_id=at(z, other % 4, x, other // 4), device_id_type=MESH)
    pl.semaphore_wait(barrier, 64 + VIEWS - 1 - first)

    def scatter(array, step, target):
        for far in (0, 8):
            z2 = (z + step + far) % 16
            for dx in range(4):
                x2 = (x + dx) % 4
                pair = z2 * 4 + x2
                own = step == 0 if (far, dx) == (0, 0) else False
                target(place(array, pair // GROUPS, pair % GROUPS), z2, x2, own)

    for which, (array, buffer) in enumerate(((key_rows, k_in), (value_rows, v_in), (queries, q_in))):

        @pl.loop(0, 8)
        def _(step):
            def target(src, z2, x2, own):
                if which == 2:
                    row = seq * TOKENS
                else:
                    row = (turn + x2) % VIEWS * SHARE + z_lo * TOKENS
                dst = buffer.at[rows(row, TOKENS)]
                here = q_here.at[z_lo] if which == 2 else in_here.at[which]
                send(src, dst, in_sent.at[which], here, at(z2, y, x2, z_hi), False if own is False else view_stays & own)

            scatter(array, step, target)

    wait(k_in, in_here.at[0])

    tell_tokens(leave)

    @pl.loop(0, VIEWS)
    def _(i):
        share = (my_share + i) % VIEWS
        y2, c2 = combiner(share)
        send(k_in.at[rows(share * SHARE, SHARE)], k_views.at[my_view], k_sent, k_here, at(z, y2, x, c2), i == 0)

    k_a[...], k_b[...] = twin_keys(k_in[...])
    pl.semaphore_wait(leave, 64 - first)

    @pl.loop(0, VIEWS)
    def _(i):
        def target(src, z2, x2, own):
            y2, c2 = combiner((turn + x2) % VIEWS)
            dst = w_in.at[view, rows(z_lo * TOKENS, TOKENS)]
            send(src, dst, in_sent.at[3], in_here.at[3], at(z2, y2, x2, c2), False if own is False else share_stays & own)

        scatter(view_queries, i, target)

    wait(v_in, in_here.at[1])
    v_a[...], v_b[...] = values_and_ones(v_in[...])

    @pl.loop(0, VIEWS)
    def _(i):
        part = (z_lo + VIEWS - i) % VIEWS
        here = rows(part * SHARE, SHARE)
        wait(q_in.at[here], q_here.at[part])
        q_a, q_b = split_queries(q_in[here])
        o_out[here] = finish(weigh(q_a, k_a[...], v_a[...]), weigh(q_b, k_b[...], v_b[...]))
        for n in range(8):
            share = (my_share + n) % VIEWS
            y2, c2 = combiner(share)
            x2, from2 = home_of(share, part)
            send(
                o_out.at[rows(part * SHARE + (x2 * 2 + from2) * TOKENS, TOKENS)],
                o_views.at[my_view, rows(part * TOKENS, TOKENS)],
                o_sent,
                o_here,
                at(z, y2, x, c2),
                n == 0,
            )


    @pl.loop(0, VIEWS)
    def _(i):
        part = (z_lo + VIEWS - i) % VIEWS
        for n in range(8):
            x2, c2 = (x + n // 2) % 4, (core + n) % 2
            send(
                o_out.at[rows(part * SHARE + (x2 * 2 + c2) * TOKENS, TOKENS)],
                place(spatial, b, g),
                home_sent.at[0],
                home_here.at[0],
                at(core * 8 + part, y, x2, c2),
                view_stays & (i == 0) if n == 0 else False,
            )

    wait(k_views, k_here)
    wait(w_in, in_here.at[3])
    wait(o_views, o_here)
    count = VIEWS * TOKENS
    same = (
        lax.broadcasted_iota(jnp.int32, (count, count), 0) % TOKENS
        == lax.broadcasted_iota(jnp.int32, (count, count), 1) % TOKENS
    )

    def send_joined(i, high):
        part = (i // 4) * 4 + (z_lo + VIEWS - i) % 4
        x2, c2 = home_of(my_share, part)
        for n in range(4):
            y2 = (y + n) % 4
            send(
                j_out.at[4 * high + y2, rows(part * TOKENS, TOKENS)],
                place(joined, b, g),
                home_sent.at[1],
                home_here.at[1],
                at(high * 8 + part, y2, x2, c2),
                share_stays & (part == z_lo) & (z_hi == high) if n == 0 else False,
            )

    @pl.loop(0, VIEWS)
    def _(i):
        part = (i // 4) * 4 + (z_lo + VIEWS - i) % 4
        here = rows(part * TOKENS, TOKENS)
        q_1, q_2 = split_queries(w_in[:, here].reshape(count, PAIR))
        k_1, k_2 = twin_keys(k_views[:, here].reshape(count, PAIR))
        v_1, v_2 = values_and_ones(o_views[:, here].reshape(count, PAIR))
        result = finish(weigh(q_1, k_1, v_1, same), weigh(q_2, k_2, v_2, same))
        j_out[:, here] = result.reshape(VIEWS, TOKENS, PAIR)

        send_joined(i, 0)

        @pl.when(i >= LATER)
        def _():
            send_joined(i - LATER, 1)

    @pl.loop(VIEWS - LATER, VIEWS)
    def _(i):
        send_joined(i, 1)

    for which, stays in enumerate((view_stays, view_stays, view_stays, share_stays)):
        wait_sent(in_sent.at[which], stays)
    wait(q_in.at[pl.ds(0, SEQ_LEN - SHARE)], k_sent)
    wait(q_in.at[pl.ds(0, SEQ_LEN - SHARE)], o_sent)
    wait_sent(home_sent.at[0], view_stays)
    wait_sent(home_sent.at[1], share_stays)
    wait(spatial, home_here.at[0])
    wait(joined, home_here.at[1])


def local(queries, key_rows, value_rows, view_queries):
    whole, shares = (SEQ_LEN, PAIR), (VIEWS, SHARE, PAIR)
    return pl.pallas_call(
        kernel,
        out_shape=[jax.ShapeDtypeStruct(queries.shape, BF16)] * 2,
        in_specs=[pl.BlockSpec(memory_space=pl.ANY)] * 4,
        out_specs=[pl.BlockSpec(memory_space=pl.ANY)] * 2,
        scratch_shapes=[
            *[pltpu.VMEM(whole, BF16)] * 3,
            pltpu.VMEM(shares, BF16),
            *[pltpu.VMEM(whole, BF16)] * 5,
            *[pltpu.VMEM(shares, BF16)] * 3,
            pltpu.SemaphoreType.DMA((4,)),
            pltpu.SemaphoreType.DMA((4,)),
            pltpu.SemaphoreType.DMA((VIEWS,)),
            pltpu.SemaphoreType.REGULAR,
            *[pltpu.SemaphoreType.DMA] * 4,
            pltpu.SemaphoreType.DMA((2,)),
            pltpu.SemaphoreType.DMA((2,)),
        ],
        compiler_params=pltpu.CompilerParams(
            collective_id=0, has_side_effects=True, vmem_limit_bytes=105 << 19
        ),
        cost_estimate=pl.CostEstimate(flops=1 << 32, bytes_accessed=1 << 22, transcendentals=1 << 23),
    )(queries, key_rows, value_rows, view_queries)


def solution(mesh):
    placed = P(None, "view", "seq", None)
    return jax.shard_map(
        local, mesh=mesh, in_specs=(placed,) * 4, out_specs=(placed, placed), check_vma=False
    )
```

```python
import jax
import jax.numpy as jnp
from jax import lax
from jax.experimental import pallas as pl
from jax.experimental.pallas import tpu as pltpu
from jax.sharding import PartitionSpec as P

MESH = pl.DeviceIdType.MESH
BF16, F32 = jnp.bfloat16, jnp.float32
BATCH, VIEWS, SEQ_LEN, D = 4, 8, 2048, 2048
TOKENS = 32
PAIR = 128
HALF = 64
GROUPS = D // PAIR
SHARE = SEQ_LEN // VIEWS
LATER = 6
SCALE = 0.125 * 1.4426950408889634


def rows(start, size):
    return pl.ds(pl.multiple_of(start, TOKENS), size)


def low_lanes(count):
    return lax.broadcasted_iota(jnp.int32, (count, PAIR), 1) < HALF


def split_queries(block):
    low = low_lanes(block.shape[0])
    scaled = block.astype(F32) * SCALE
    first = scaled.astype(BF16).astype(F32)
    second = pltpu.roll(scaled - first, HALF, 1)
    return jnp.where(low, first, second).astype(BF16), jnp.where(low, second, first).astype(BF16)


def twin_keys(block):
    low = low_lanes(block.shape[0])
    plain = block.astype(F32)
    moved = pltpu.roll(plain, HALF, 1)
    return jnp.where(low, plain, moved).astype(BF16), jnp.where(low, moved, plain).astype(BF16)


def values_and_ones(block):
    low = low_lanes(block.shape[0])
    plain = block.astype(F32)
    return jnp.where(low, plain, 1.0).astype(BF16), jnp.where(low, 1.0, plain).astype(BF16)


def weigh(query, key, value, mask=None):
    scores = lax.dot_general(query, key, (((1,), (1,)), ((), ())), preferred_element_type=F32)
    if mask is not None:
        scores = jnp.where(mask, scores, -1e30)
    scores = scores - jnp.max(scores, axis=1, keepdims=True)
    return jnp.dot(jnp.exp2(scores).astype(BF16), value, preferred_element_type=F32)


def finish(first, second):
    low = low_lanes(first.shape[0])
    total = pltpu.roll(jnp.where(low, second, first), HALF, 1)
    return (jnp.where(low, first, second) / total).astype(BF16)


def kernel(
    queries, key_rows, value_rows, view_queries, spatial, joined,
    k_in, v_in, q_in, w_in, k_a, k_b, v_a, v_b, o_out, k_views, o_views, j_out,
    in_sent, in_here, q_here, leave, k_sent, k_here, o_sent, o_here, home_sent, home_here,
):
    view, seq = lax.axis_index("view"), lax.axis_index("seq")
    z_hi, y = view // 4, view % 4
    z_lo, x, core = seq // 8, (seq // 2) % 4, seq % 2
    z = z_hi * 8 + z_lo
    my_pair = z * 4 + x
    my_view = core * 4 + y
    b, g = my_pair // GROUPS, my_pair % GROUPS
    view_stays = z_hi == core
    my_share = (y % 2) + 2 * core + 4 * (y // 2)
    turn = z_lo + x + 4 * core
    share_stays = (turn + x) % VIEWS == my_share

    def at(z, y, x, core):
        return ((z // 8) * 4 + y, (z % 8) * 8 + x * 2 + core)

    def combiner(share):
        return (share % 2) + 2 * (share // 4), (share // 2) % 2

    def home_of(share, part):
        turn = (share - x - part + 2 * VIEWS) % VIEWS
        return turn % 4, turn // 4

    def place(ref, b, g):
        return ref.at[b, 0, :, pl.ds(pl.multiple_of(g * PAIR, PAIR), PAIR)]

    def send(src, dst, sent, here, device, stays):
        if stays is False:
            pltpu.make_async_remote_copy(src, dst, sent, here, device_id=device, device_id_type=MESH).start()
            return

        if stays is True:
            pltpu.make_async_copy(src, dst, here).start()
            return

        @pl.when(jnp.logical_not(stays))
        def _():
            pltpu.make_async_remote_copy(src, dst, sent, here, device_id=device, device_id_type=MESH).start()

        @pl.when(stays)
        def _():
            pltpu.make_async_copy(src, dst, here).start()

    def wait(ref, sem):
        pltpu.make_async_copy(ref, ref, sem).wait()

    def wait_sent(sem, stays):
        @pl.when(stays)
        def _():
            wait(q_in.at[pl.ds(0, SEQ_LEN - TOKENS)], sem)

        @pl.when(jnp.logical_not(stays))
        def _():
            wait(q_in, sem)

    barrier = pltpu.get_barrier_semaphore()
    first = view_stays.astype(jnp.int32)

    def tell_tokens(sem):
        @pl.when(jnp.logical_not(view_stays))
        def _():
            pl.semaphore_signal(sem, inc=1, device_id=(my_view, seq), device_id_type=MESH)

        @pl.loop(1, 64, unroll=9)
        def _(i):
            pl.semaphore_signal(sem, inc=1, device_id=(my_view, lax.rem(seq + i, 64)), device_id_type=MESH)

    tell_tokens(barrier)

    for i in range(1, VIEWS):
        other = (my_view + i) % VIEWS
        pl.semaphore_signal(barrier, inc=1, device_id=at(z, other % 4, x, other // 4), device_id_type=MESH)
    pl.semaphore_wait(barrier, 64 + VIEWS - 1 - first)

    def scatter(array, step, target):
        for far in (0, 8):
            z2 = (z + step + far) % 16
            for dx in range(4):
                x2 = (x + dx) % 4
                pair = z2 * 4 + x2
                own = step == 0 if (far, dx) == (0, 0) else False
                target(place(array, pair // GROUPS, pair % GROUPS), z2, x2, own)

    for which, (array, buffer) in enumerate(((key_rows, k_in), (value_rows, v_in), (queries, q_in))):

        @pl.loop(0, 8)
        def _(step):
            def target(src, z2, x2, own):
                if which == 2:
                    row = seq * TOKENS
                else:
                    row = (turn + x2) % VIEWS * SHARE + z_lo * TOKENS
                dst = buffer.at[rows(row, TOKENS)]
                here = q_here.at[z_lo] if which == 2 else in_here.at[which]
                send(src, dst, in_sent.at[which], here, at(z2, y, x2, z_hi), False if own is False else view_stays & own)

            scatter(array, step, target)

    wait(k_in, in_here.at[0])

    tell_tokens(leave)

    @pl.loop(0, VIEWS)
    def _(i):
        share = (my_share + i) % VIEWS
        y2, c2 = combiner(share)
        send(k_in.at[rows(share * SHARE, SHARE)], k_views.at[my_view], k_sent, k_here, at(z, y2, x, c2), i == 0)

    k_a[...], k_b[...] = twin_keys(k_in[...])
    pl.semaphore_wait(leave, 64 - first)

    @pl.loop(0, VIEWS)
    def _(i):
        def target(src, z2, x2, own):
            y2, c2 = combiner((turn + x2) % VIEWS)
            dst = w_in.at[view, rows(z_lo * TOKENS, TOKENS)]
            send(src, dst, in_sent.at[3], in_here.at[3], at(z2, y2, x2, c2), False if own is False else share_stays & own)

        scatter(view_queries, i, target)

    wait(v_in, in_here.at[1])
    v_a[...], v_b[...] = values_and_ones(v_in[...])

    @pl.loop(0, VIEWS)
    def _(i):
        part = (z_lo + VIEWS - i) % VIEWS
        here = rows(part * SHARE, SHARE)
        wait(q_in.at[here], q_here.at[part])
        q_a, q_b = split_queries(q_in[here])
        o_out[here] = finish(weigh(q_a, k_a[...], v_a[...]), weigh(q_b, k_b[...], v_b[...]))
        for n in range(8):
            share = (my_share + n) % VIEWS
            y2, c2 = combiner(share)
            x2, from2 = home_of(share, part)
            send(
                o_out.at[rows(part * SHARE + (x2 * 2 + from2) * TOKENS, TOKENS)],
                o_views.at[my_view, rows(part * TOKENS, TOKENS)],
                o_sent,
                o_here,
                at(z, y2, x, c2),
                n == 0,
            )


    @pl.loop(0, VIEWS)
    def _(i):
        part = (z_lo + VIEWS - i) % VIEWS
        for n in range(8):
            x2, c2 = (x + n // 2) % 4, (core + n) % 2
            send(
                o_out.at[rows(part * SHARE + (x2 * 2 + c2) * TOKENS, TOKENS)],
                place(spatial, b, g),
                home_sent.at[0],
                home_here.at[0],
                at(core * 8 + part, y, x2, c2),
                view_stays & (i == 0) if n == 0 else False,
            )

    wait(k_views, k_here)
    wait(w_in, in_here.at[3])
    wait(o_views, o_here)
    count = VIEWS * TOKENS
    same = (
        lax.broadcasted_iota(jnp.int32, (count, count), 0) % TOKENS
        == lax.broadcasted_iota(jnp.int32, (count, count), 1) % TOKENS
    )

    def send_joined(i, high):
        part = (i // 2) * 2 + (z_lo + VIEWS - i) % 2
        x2, c2 = home_of(my_share, part)
        for n in range(4):
            y2 = (y + n) % 4
            send(
                j_out.at[4 * high + y2, rows(part * TOKENS, TOKENS)],
                place(joined, b, g),
                home_sent.at[1],
                home_here.at[1],
                at(high * 8 + part, y2, x2, c2),
                share_stays & (part == z_lo) & (z_hi == high) if n == 0 else False,
            )

    @pl.loop(0, VIEWS)
    def _(i):
        part = (i // 2) * 2 + (z_lo + VIEWS - i) % 2
        here = rows(part * TOKENS, TOKENS)
        q_1, q_2 = split_queries(w_in[:, here].reshape(count, PAIR))
        k_1, k_2 = twin_keys(k_views[:, here].reshape(count, PAIR))
        v_1, v_2 = values_and_ones(o_views[:, here].reshape(count, PAIR))
        result = finish(weigh(q_1, k_1, v_1, same), weigh(q_2, k_2, v_2, same))
        j_out[:, here] = result.reshape(VIEWS, TOKENS, PAIR)

        send_joined(i, 0)

        @pl.when(i >= LATER)
        def _():
            send_joined(i - LATER, 1)

    @pl.loop(VIEWS - LATER, VIEWS)
    def _(i):
        send_joined(i, 1)

    for which, stays in enumerate((view_stays, view_stays, view_stays, share_stays)):
        wait_sent(in_sent.at[which], stays)
    wait(q_in.at[pl.ds(0, SEQ_LEN - SHARE)], k_sent)
    wait(q_in.at[pl.ds(0, SEQ_LEN - SHARE)], o_sent)
    wait_sent(home_sent.at[0], view_stays)
    wait_sent(home_sent.at[1], share_stays)
    wait(spatial, home_here.at[0])
    wait(joined, home_here.at[1])


def local(queries, key_rows, value_rows, view_queries):
    whole, shares = (SEQ_LEN, PAIR), (VIEWS, SHARE, PAIR)
    return pl.pallas_call(
        kernel,
        out_shape=[jax.ShapeDtypeStruct(queries.shape, BF16)] * 2,
        in_specs=[pl.BlockSpec(memory_space=pl.ANY)] * 4,
        out_specs=[pl.BlockSpec(memory_space=pl.ANY)] * 2,
        scratch_shapes=[
            *[pltpu.VMEM(whole, BF16)] * 3,
            pltpu.VMEM(shares, BF16),
            *[pltpu.VMEM(whole, BF16)] * 5,
            *[pltpu.VMEM(shares, BF16)] * 3,
            pltpu.SemaphoreType.DMA((4,)),
            pltpu.SemaphoreType.DMA((4,)),
            pltpu.SemaphoreType.DMA((VIEWS,)),
            pltpu.SemaphoreType.REGULAR,
            *[pltpu.SemaphoreType.DMA] * 4,
            pltpu.SemaphoreType.DMA((2,)),
            pltpu.SemaphoreType.DMA((2,)),
        ],
        compiler_params=pltpu.CompilerParams(
            collective_id=0, has_side_effects=True, vmem_limit_bytes=105 << 19
        ),
        cost_estimate=pl.CostEstimate(flops=1 << 32, bytes_accessed=1 << 22, transcendentals=1 << 23),
    )(queries, key_rows, value_rows, view_queries)


def solution(mesh):
    placed = P(None, "view", "seq", None)
    return jax.shard_map(
        local, mesh=mesh, in_specs=(placed,) * 4, out_specs=(placed, placed), check_vma=False
    )
```
